256 devices in a mesh: blk: 128 (over y_hi, z, x, core), rep: 2 (over y_lo).
Axes of the slice: x: 4, y: 4 (y_hi: 2, y_lo: 2; y = y_hi * 2 + y_lo), z: 8, core: 2. Of those that a mesh axis runs over, the one named last changes fastest.
Arguments:
- features: float32 [32768, 256], P('blk', 'rep'), may hold values from -6 to 6
- scaling: float32 [32768], P('blk'), may hold values from 0.5 to 2
- signal: float32 [64, 32768], P('rep', 'blk'), may hold values from -6 to 6
Outputs:
- diffused: float32 [64, 32768], P('rep', 'blk')
The draws below stay inside these ranges and needn't reach their ends.
All inputs are finite; a program needn't handle non-finite values.
Results may differ from the reference program's by a relative error of at most 0.0003.
Values sent between devices are 32-bit elements; how exact they have to be, the bound alone decides.
No kernel may reach another device: no remote copies, remote signals or barrier semaphores. Data moves between devices by JAX's collectives and lax.ppermute only.
A program may use at most 64 MiB of HBM per device.

```python
import math
import jax
import jax.numpy as jnp
from jax import lax

CELLS_DEV = 256
DIM = 256
COLS = 64
CELLS = 32768
N_BLK = 128


def block_scale(key, extent, pieces, smallest, high):
    loudness, own = 1.0, jax.random.fold_in(key, 6)
    for dim, blocks in pieces:
        steps = jnp.exp(jax.random.uniform(jax.random.fold_in(own, dim), (blocks,), jnp.float32, smallest / len(pieces), high / len(pieces)))
        loudness = loudness * jnp.repeat(steps, extent[dim] // blocks).reshape([-1 if axis == dim else 1 for axis in range(len(extent))])
    return loudness


def centred(key, dims, deviation, most, cuts=(), kind=jnp.bfloat16):
    level = block_scale(key, dims, cuts, -0.22, 0.18) if cuts else 1.0
    result = jax.random.normal(key, dims, jnp.float32) * deviation * level
    return jnp.minimum(jnp.maximum(result, -most), most).astype(kind)


def setup_inputs(seed: int = 0) -> dict:
    key_of = jax.random.split(jax.random.key(seed), 4)
    return {
        "features": centred(key_of[0], (CELLS, DIM), 1.0, 6.0, ((0, 128), (1, 2)), jnp.float32),
        "scaling": jnp.clip(jnp.exp(math.log(2.0) - 1.3862944 * jax.random.uniform(key_of[1], (CELLS,), jnp.float32) ** block_scale(key_of[1], (CELLS,), ((0, 128),), -0.2, 0.2)), 0.5, 2.0),
        "signal": centred(key_of[2], (COLS, CELLS), 1.0, 6.0, ((0, 2), (1, 128)), jnp.float32),
    }


HIGH = lax.Precision.HIGHEST
SHARPNESS = 48.0

def scaled(full):
    mean_square = lax.optimization_barrier(jnp.mean(full * full, axis=1, keepdims=True))
    return full * lax.rsqrt(mean_square + 1e-06) * math.sqrt(SHARPNESS / full.shape[1])

def kernel_tile(left, right):
    inner = lax.dot_general(left, right, (((1,), (1,)), ((), ())), precision=HIGH, preferred_element_type=jnp.float32)
    return jnp.exp(inner)

def reference(features, scaling, signal):
    unit = scaled(features)
    cells = unit.shape[0]

    def block_kernel(index):
        rows = lax.dynamic_slice_in_dim(unit, index * CELLS_DEV, CELLS_DEV, 0)
        kern = kernel_tile(rows, unit)
        row_ids = index * CELLS_DEV + lax.broadcasted_iota(jnp.int32, (CELLS_DEV, cells), 0)
        col_ids = lax.broadcasted_iota(jnp.int32, (CELLS_DEV, cells), 1)
        return jnp.where(row_ids == col_ids, jnp.float32(0.0), kern)

    def first(index):
        return jnp.dot(block_kernel(index), scaling, precision=HIGH, preferred_element_type=jnp.float32)
    sums = lax.map(first, jnp.arange(N_BLK, dtype=jnp.int32)).reshape(cells)
    balanced = jnp.sqrt(scaling / sums)
    weighted = signal * balanced[None, :]

    def second(index):
        kern = block_kernel(index)
        return lax.dot_general(weighted, kern, (((1,), (1,)), ((), ())), precision=HIGH, preferred_element_type=jnp.float32)
    parts = lax.map(second, jnp.arange(N_BLK, dtype=jnp.int32))
    diffused = jnp.transpose(parts, (1, 0, 2)).reshape(COLS, cells)
    return diffused * balanced[None, :]
```

```python
import functools
import math

import jax
import jax.numpy as jnp
from jax import lax
from jax.experimental import pallas as pl
from jax.experimental.pallas import tpu as pltpu
from jax.sharding import Mesh
from jax.sharding import PartitionSpec as P

F32, BF16 = jnp.float32, jnp.bfloat16
LOG2E = 1.4426950408889634
SHARPNESS = 48.0
NT = (((1,), (1,)), ((), ()))
NN = (((1,), (0,)), ((), ()))
SM = pl.BlockSpec(memory_space=pltpu.SMEM)
AXES = ("yh", "z", "x", "co", "yl")
PLANE = ("yh", "x", "yl")
LINE = ("z", "co")
EXTRA = 40


def params(mib):
    return pltpu.CompilerParams(vmem_limit_bytes=mib * 2**20)


def split(value):
    high = value.astype(BF16)
    return high, (value - high.astype(F32)).astype(BF16)


def unit(full):
    mean_square = jnp.mean(full * full, axis=1, keepdims=True)
    return full * (lax.rsqrt(mean_square + 1e-06) * math.sqrt(SHARPNESS / full.shape[1]))


def rows_kernel(got_ref, rows_ref, scale_ref):
    full = jnp.concatenate([got_ref[0, 0:256, :], got_ref[1, 0:256, :]], axis=1)
    high, low = split(unit(full))
    rows_ref[:, 0:256] = high
    rows_ref[:, 256:512] = low
    rows_ref[:, 512:768] = high
    for h in range(2):
        scale = got_ref[0, 256 + h : 257 + h, :]
        scale_ref[h * 128 : (h + 1) * 128, :] = jnp.broadcast_to(scale, (128, 128)).T


def prepare_rows(got):
    return pl.pallas_call(
        rows_kernel,
        grid=(8,),
        in_specs=[pl.BlockSpec((2, 264, 128), lambda i: (i, 0, 0))],
        out_specs=[
            pl.BlockSpec((256, 768), lambda i: (i, 0)),
            pl.BlockSpec((256, 128), lambda i: (i, 0)),
        ],
        out_shape=[
            jax.ShapeDtypeStruct((2048, 768), BF16),
            jax.ShapeDtypeStruct((2048, 128), F32),
        ],
        compiler_params=params(12),
        cost_estimate=pl.CostEstimate(flops=3_000_000, bytes_accessed=6_400_000, transcendentals=0),
        name="prepare_rows",
    )(got)


def tile_kernel(has_self, tn, place_ref, rows_ref, cols_ref, scale_ref, kh_ref, kl_ref, sum_ref, unit_ref, acc_ref):
    tm = rows_ref.shape[0]
    count = unit_ref.shape[0]
    i = pl.program_id(0)

    @pl.when(i == 0)
    def _():
        for b in range(8):
            high, low = split(unit(cols_ref[b, EXTRA:, :]) * LOG2E)
            rows = pl.ds(pl.multiple_of(place_ref[3 + b] * 128, 128), 128)
            unit_ref[rows, 0:256] = high
            unit_ref[rows, 256:512] = high
            unit_ref[rows, 512:768] = low
        acc_ref[...] = jnp.zeros_like(acc_ref)

    def step(masked):
        scale = scale_ref[...]
        for j in range(count // tn):
            inner = lax.dot_general(
                rows_ref[...], unit_ref[j * tn : (j + 1) * tn, :], NT, preferred_element_type=F32
            )
            kern = jnp.exp2(inner)
            if masked:
                row = lax.broadcasted_iota(jnp.int32, (tm, tn), 0) + (i * tm - place_ref[0])
                col = lax.broadcasted_iota(jnp.int32, (tm, tn), 1) + (j * tn - place_ref[1])
                kern = jnp.where((row == col) & (col >= 0) & (col < 128), 0.0, kern)
            high, low = split(kern)
            kh_ref[:, j * tn : (j + 1) * tn] = high
            kl_ref[:, j * tn : (j + 1) * tn] = low
            for q in range(tn // 128):
                part = kern[:, q * 128 : (q + 1) * 128] * scale
                lanes = slice(j * tn + q * 128, j * tn + (q + 1) * 128)
                acc_ref[:, lanes] += part.reshape(tm // 8, 8, 128).sum(0)

    if has_self:
        pl.when(i == place_ref[2])(lambda: step(True))
        pl.when(i != place_ref[2])(lambda: step(False))
    else:
        step(False)

    @pl.when(i == pl.num_programs(0) - 1)
    def _():
        for b in range(8):
            sum_ref[b : b + 1, :] = acc_ref[:, b * 128 : (b + 1) * 128].sum(0, keepdims=True)


def tile(place, rows, cols, scale, has_self, tm=512, tn=256):
    return pl.pallas_call(
        functools.partial(tile_kernel, has_self, tn),
        grid=(2048 // tm,),
        in_specs=[
            SM,
            pl.BlockSpec((tm, 768), lambda i: (i, 0)),
            pl.BlockSpec((8, EXTRA + 128, 256), lambda i: (0, 0, 0)),
            pl.BlockSpec((tm, 128), lambda i: (i, 0)),
        ],
        out_specs=[
            pl.BlockSpec((tm, 1024), lambda i: (i, 0)),
            pl.BlockSpec((tm, 1024), lambda i: (i, 0)),
            pl.BlockSpec((8, 128), lambda i: (0, 0)),
        ],
        out_shape=[pltpu.HBM((2048, 1024), BF16)] * 2
        + [jax.ShapeDtypeStruct((8, 128), F32)],
        scratch_shapes=[pltpu.VMEM((1024, 768), BF16), pltpu.VMEM((8, 1024), F32)],
        compiler_params=params(14),
        cost_estimate=pl.CostEstimate(flops=3_200_000_000, bytes_accessed=14_000_000, transcendentals=2_000_000),
        name="tile_self" if has_self else "tile_plain",
    )(place, rows, cols, scale)


def diffuse_kernel(place_ref, sum0, sum1, extra0, extra1, kh0, kl0, kh1, kl1, out_ref, weight_ref, held, sems):
    depth = held.shape[0]
    steps = kh0.shape[0] // 256

    def fetch(i):
        return [
            pltpu.make_async_copy(k.at[pl.ds(i * 256, 256)], held.at[i % depth, n], sems.at[i % depth, n])
            for n, k in enumerate((kh0, kh1, kl0, kl1))
        ]

    for i in range(depth):
        for copy in fetch(i):
            copy.start()
    for core, (sums, extra) in enumerate(((sum0, extra0), (sum1, extra1))):
        for b in range(8):
            at = place_ref[3 + b]
            balanced = jnp.sqrt(extra[b, 32:33, 0:128] / sums[pl.ds(at, 1), :])
            signal = jnp.concatenate([extra[b, 0:32, 0:128], extra[b, 0:32, 128:256]], axis=0)
            weight = signal * balanced
            lead = weight.astype(BF16).astype(F32)
            both = jnp.concatenate([lead, weight - lead], axis=0).T.astype(BF16)
            start = pl.multiple_of(core * 1024 + at * 128, 128)
            weight_ref[pl.ds(start, 128), :] = both
    near, far = weight_ref[0:1024, :], weight_ref[1024:2048, :]
    for i in range(steps):
        for copy in fetch(i):
            copy.wait()
        slot = i % depth
        lead = lax.dot_general(held[slot, 0], near, NN, preferred_element_type=F32)
        lead += lax.dot_general(held[slot, 1], far, NN, preferred_element_type=F32)
        rest = lax.dot_general(held[slot, 2], near[:, :64], NN, preferred_element_type=F32)
        rest += lax.dot_general(held[slot, 3], far[:, :64], NN, preferred_element_type=F32)
        total = (lead[:, :64] + lead[:, 64:] + rest).T
        out_ref[2 * i] = total[:32]
        out_ref[2 * i + 1] = total[32:]
        if i + depth < steps:
            for copy in fetch(i + depth):
                copy.start()


def diffuse(place, sum0, sum1, cols0, cols1, kh0, kl0, kh1, kl1):
    small = pl.BlockSpec((8, 128), lambda i: (0, 0))
    extra = pl.BlockSpec((8, EXTRA, 256), lambda i: (0, 0, 0))
    kern = pl.BlockSpec(memory_space=pltpu.HBM)
    return pl.pallas_call(
        diffuse_kernel,
        grid=(1,),
        in_specs=[SM, small, small, extra, extra, kern, kern, kern, kern],
        out_specs=pl.BlockSpec((16, 32, 256), lambda i: (0, 0, 0)),
        out_shape=jax.ShapeDtypeStruct((16, 32, 256), F32),
        scratch_shapes=[
            pltpu.VMEM((2048, 128), BF16),
            pltpu.VMEM((4, 4, 256, 1024), BF16),
            pltpu.SemaphoreType.DMA((4, 4)),
        ],
        compiler_params=params(60),
        cost_estimate=pl.CostEstimate(flops=3_200_000_000, bytes_accessed=18_000_000, transcendentals=0),
        name="diffuse",
    )(place, sum0, sum1, cols0, cols1, kh0, kl0, kh1, kl1)


def swapped(array, axis):
    return lax.ppermute(array, axis, [(0, 1), (1, 0)])


def to_all(array, axes, count):
    spread = jnp.broadcast_to(array[None], (count,) + array.shape)
    return lax.all_to_all(spread, axes, 0, 0, tiled=True)


def shifted(array, axis, by):
    length = lax.axis_size(axis)
    return lax.ppermute(array, axis, [(i, (i + by) % length) for i in range(length)])


def on_device(features, scaling, signal):
    yh, z, x, co, yl = (lax.axis_index(a) for a in AXES)
    lower, first_core = yl == 0, co == 0

    def ordered(is_first, a, b, axis):
        return jnp.concatenate([jnp.where(is_first, a, b), jnp.where(is_first, b, a)], axis=axis)

    message = jnp.concatenate([features, scaling.reshape(2, 128), jnp.zeros((6, 128), F32)], axis=0)
    rows_raw = to_all(message, PLANE, 16)

    give = jnp.where(
        lower,
        jnp.concatenate([signal[:, 128:], features[128:]], axis=0),
        jnp.concatenate([signal[:, :128], features[:128]], axis=0),
    )
    kept = jnp.where(
        lower,
        jnp.concatenate([signal[:, :128], features[:128]], axis=0),
        jnp.concatenate([signal[:, 128:], features[128:]], axis=0),
    )
    got = swapped(give, "yl")
    own_scaling = jnp.where(lower, scaling[:128], scaling[128:])
    both = ordered(lower, kept, got, 1)
    filler = jnp.zeros((EXTRA - 32, 256), F32).at[0, :128].set(own_scaling)
    own = jnp.concatenate([both[:32], filler, both[32:]], axis=0)[None]

    opposite = shifted(own, "z", 4)
    ahead, behind = shifted(own, "z", 2), shifted(own, "z", -2)
    pair = jnp.concatenate([own, opposite], axis=0)
    up, down = shifted(pair, "z", 1), shifted(pair, "z", -1)
    cols_near = jnp.concatenate([pair, ahead, behind, up, down], axis=0)
    cols_far = swapped(cols_near, "co")
    offsets = (0, 4, -2, 2, -1, 3, 1, 5)

    rows, scale = prepare_rows(rows_raw)
    row_at = (yh * 4 + x) * 256 + yl * 128
    place = jnp.stack([row_at, z * 128, row_at // 512] + [(z + o) % 8 for o in offsets]).astype(jnp.int32)
    kh0, kl0, sum0 = tile(place, rows, cols_near, scale, True)
    kh1, kl1, sum1 = tile(place, rows, cols_far, scale, False)

    parts = to_all(ordered(first_core, sum0, sum1, 0), LINE, 16)
    sums = parts.sum(0)
    sum0 = jnp.where(first_core, sums[:8], sums[8:])
    sum1 = jnp.where(first_core, sums[8:], sums[:8])
    own_balanced = jnp.sqrt(own_scaling[None] / lax.dynamic_slice(sum0, (z, 0), (1, 128)))
    other_balanced = swapped(own_balanced, "yl")
    terms = diffuse(place, sum0, sum1, cols_near, cols_far, kh0, kl0, kh1, kl1)
    arrived = lax.all_to_all(terms, PLANE, 0, 0, tiled=True)
    return arrived.sum(0) * ordered(lower, own_balanced, other_balanced, 1)


def solution(mesh):
    fine = Mesh(mesh.devices.reshape(2, 8, 4, 2, 2), AXES)
    blk = ("yh", "z", "x", "co")
    return jax.shard_map(
        on_device,
        mesh=fine,
        in_specs=(P(blk, "yl"), P(blk), P("yl", blk)),
        out_specs=P("yl", blk),
        check_vma=False,
    )
```

```python
import functools
import math

import jax
import jax.numpy as jnp
from jax import lax
from jax.experimental import pallas as pl
from jax.experimental.pallas import tpu as pltpu
from jax.sharding import Mesh
from jax.sharding import PartitionSpec as P

F32, BF16 = jnp.float32, jnp.bfloat16
LOG2E = 1.4426950408889634
SHARPNESS = 48.0
NT = (((1,), (1,)), ((), ()))
NN = (((1,), (0,)), ((), ()))
SM = pl.BlockSpec(memory_space=pltpu.SMEM)
AXES = ("yh", "z", "x", "co", "yl")
PLANE = ("yh", "x", "yl")
LINE = ("z", "co")
EXTRA = 40


def params(mib):
    return pltpu.CompilerParams(vmem_limit_bytes=mib * 2**20)


def split(value):
    high = value.astype(BF16)
    return high, (value - high.astype(F32)).astype(BF16)


def unit(full):
    mean_square = jnp.mean(full * full, axis=1, keepdims=True)
    return full * (lax.rsqrt(mean_square + 1e-06) * math.sqrt(SHARPNESS / full.shape[1]))


def whole(*shape):
    return pl.BlockSpec(shape, lambda i: (0,) * len(shape))


def share_kernel(features_ref, signal_ref, give_ref, kept_ref):
    place = lax.axis_index("yl")
    for own in range(2):

        @pl.when(place == own)
        def _():
            for half, out in ((own, kept_ref), (1 - own, give_ref)):
                out[0:32, :] = signal_ref[:, half * 128 : (half + 1) * 128]
                out[32:160, :] = features_ref[half * 128 : (half + 1) * 128, :]


def share(features, signal):
    return pl.pallas_call(
        share_kernel,
        grid=(1,),
        in_specs=[whole(256, 128), whole(32, 256)],
        out_specs=[whole(160, 128)] * 2,
        out_shape=[jax.ShapeDtypeStruct((160, 128), F32)] * 2,
        compiler_params=params(62),
        cost_estimate=pl.CostEstimate(flops=100_000, bytes_accessed=300_000, transcendentals=0),
        name="share",
    )(features, signal)


def pack_kernel(features_ref, scaling_ref, after_ref, spread_ref):
    for n in range(16):
        spread_ref[n, 0:256, :] = features_ref[...]
        spread_ref[n, 256:258, :] = scaling_ref[...]
        spread_ref[n, 258:264, :] = jnp.zeros((6, 128), F32)


def pack(features, scaling, after):
    return pl.pallas_call(
        pack_kernel,
        grid=(1,),
        in_specs=[whole(256, 128), whole(2, 128), pl.BlockSpec(memory_space=pl.ANY)],
        out_specs=whole(16, 264, 128),
        out_shape=jax.ShapeDtypeStruct((16, 264, 128), F32),
        compiler_params=params(62),
        cost_estimate=pl.CostEstimate(flops=100_000, bytes_accessed=2_500_000, transcendentals=0),
        name="pack",
    )(features, scaling, after)


def block_rows(first, second):
    high, low = split(unit(jnp.concatenate([first[0:256, :], second[0:256, :]], axis=1)))
    return jnp.concatenate([high, low, high], axis=1)


def rows_kernel(got_ref, rows_ref, scale_ref):
    i = pl.program_id(0)
    rows_ref[...] = block_rows(got_ref[0], got_ref[1])
    for h in range(2):
        scale_ref[pl.ds(2 * i + h, 1), :] = got_ref[0, 256 + h : 257 + h, :]


def prepare_rows(got):
    return pl.pallas_call(
        rows_kernel,
        grid=(8,),
        in_specs=[pl.BlockSpec((2, 264, 128), lambda i: (i, 0, 0))],
        out_specs=[pl.BlockSpec((256, 768), lambda i: (i, 0)), whole(16, 128)],
        out_shape=[
            jax.ShapeDtypeStruct((2048, 768), BF16),
            jax.ShapeDtypeStruct((16, 128), F32),
        ],
        compiler_params=params(12),
        cost_estimate=pl.CostEstimate(flops=3_000_000, bytes_accessed=6_400_000, transcendentals=0),
        name="prepare_rows",
    )(got)


def kernel_of(units, rows, own=None):
    kern = jnp.exp2(lax.dot_general(units, rows, NT, preferred_element_type=F32))
    if own is None:
        return kern
    col = lax.broadcasted_iota(jnp.int32, (128, 256), 0)
    row = lax.broadcasted_iota(jnp.int32, (128, 256), 1) - own
    return jnp.concatenate([jnp.where(row == col, 0.0, kern[:128]), kern[128:]], axis=0)


def tile_columns(place_ref, rows_ref, cols_ref, scale_ref, unit_ref, acc_ref, has_self):
    for b in range(8):
        high, low = split(unit(cols_ref[b, EXTRA:, :]) * LOG2E)
        at = slice(b * 128, (b + 1) * 128)
        unit_ref[at, 0:256] = high
        unit_ref[at, 256:512] = high
        unit_ref[at, 512:768] = low
    for c in range(8):
        rows = rows_ref[c * 256 : (c + 1) * 256, :]
        kern = kernel_of(unit_ref[...], rows, place_ref[0] - c * 256 if has_self else None)
        part = kern[:, :128] * scale_ref[2 * c : 2 * c + 1, :]
        part += kern[:, 128:] * scale_ref[2 * c + 1 : 2 * c + 2, :]
        acc_ref[...] = part if c == 0 else acc_ref[...] + part
    total = lax.dot_general(
        jnp.ones((8, 128), F32), acc_ref[...], NT, precision=lax.Precision.HIGHEST, preferred_element_type=F32
    )
    return [total[0:1, b * 128 : (b + 1) * 128] for b in range(8)]


def near_kernel(place_ref, rows_ref, cols_ref, scale_ref, unit_ref, sum_ref, acc_ref):
    sums = tile_columns(place_ref, rows_ref, cols_ref, scale_ref, unit_ref, acc_ref, True)
    for b in range(8):
        sum_ref[b : b + 1, :] = sums[b]


def far_kernel(place_ref, rows_ref, cols_ref, scale_ref, near_ref, unit_ref, spread_ref, acc_ref):
    sums = tile_columns(place_ref, rows_ref, cols_ref, scale_ref, unit_ref, acc_ref, False)
    first = place_ref[1] * 8
    for b in range(8):
        spread_ref[0, pl.ds(first + place_ref[2 + b], 1), :] = near_ref[b : b + 1, :]
        spread_ref[0, pl.ds(8 - first + place_ref[2 + b], 1), :] = sums[b]
    for n in range(1, 16):
        spread_ref[n] = spread_ref[0]


def tile(place, rows, cols, scale, near=None):
    vm = pl.BlockSpec(memory_space=pltpu.VMEM)
    first = near is None
    return pl.pallas_call(
        near_kernel if first else far_kernel,
        in_specs=[SM] + [vm] * (3 if first else 4),
        out_specs=[vm, vm],
        out_shape=[
            jax.ShapeDtypeStruct((1024, 768), BF16),
            jax.ShapeDtypeStruct((8, 128) if first else (16, 16, 128), F32),
        ],
        scratch_shapes=[
            pltpu.VMEM((1024, 128), F32),
        ],
        compiler_params=params(16),
        cost_estimate=pl.CostEstimate(flops=3_200_000_000, bytes_accessed=14_000_000, transcendentals=2_000_000),
        name="tile_near" if first else "tile_far",
    )(place, rows, cols, scale, *([] if first else [near]))


def diffuse_kernel(
    place_ref, parts_ref, extra0, extra1, rows_ref, unit0, unit1, out_ref, balanced_ref, weight_ref, sums_ref, held
):
    sums_ref[...] = parts_ref[...].sum(0)
    first = place_ref[1] * 8
    for core, extra in enumerate((extra0, extra1)):
        base = first if core == 0 else 8 - first
        for b in range(8):
            balanced = jnp.sqrt(extra[b, 32:33, 0:128] / sums_ref[pl.ds(base + place_ref[2 + b], 1), :])
            if core == 0 and b == 0:
                balanced_ref[...] = balanced
            signal = jnp.concatenate([extra[b, 0:32, 0:128], extra[b, 0:32, 128:256]], axis=0)
            start = core * 1024 + b * 128
            for n, part in enumerate(split(signal * balanced)):
                weight_ref[n * 64 : (n + 1) * 64, start : start + 128] = part
    for c in range(9):
        if c < 8:
            rows = rows_ref[c * 256 : (c + 1) * 256, :]
            for core, units in enumerate((unit0, unit1)):
                at = slice(core * 1024, (core + 1) * 1024)
                kern = kernel_of(units[...], rows, None if core else place_ref[0] - c * 256)
                held[c % 2, 0, at, :], held[c % 2, 1, at, :] = split(kern)
        if c > 0:
            slot = (c - 1) % 2
            lead = lax.dot_general(weight_ref[...], held[slot, 0], NN, preferred_element_type=F32)
            rest = lax.dot_general(weight_ref[0:64, :], held[slot, 1], NN, preferred_element_type=F32)
            total = lead[:64] + lead[64:] + rest
            out_ref[2 * c - 2] = total[:32]
            out_ref[2 * c - 1] = total[32:]


def diffuse(place, parts, cols0, cols1, rows, unit0, unit1):
    vm = pl.BlockSpec(memory_space=pltpu.VMEM)
    return pl.pallas_call(
        diffuse_kernel,
        in_specs=[SM] + [vm] * 6,
        out_specs=[vm, vm],
        out_shape=[jax.ShapeDtypeStruct((16, 32, 256), F32), jax.ShapeDtypeStruct((1, 128), F32)],
        scratch_shapes=[
            pltpu.VMEM((128, 2048), BF16),
            pltpu.VMEM((16, 128), F32),
            pltpu.VMEM((2, 2, 2048, 256), BF16),
        ],
        compiler_params=params(28),
        cost_estimate=pl.CostEstimate(flops=3_200_000_000, bytes_accessed=18_000_000, transcendentals=0),
        name="diffuse",
    )(place, parts, cols0, cols1, rows, unit0, unit1)


def swapped(array, axis):
    return lax.ppermute(array, axis, [(0, 1), (1, 0)])


def to_all(array, axes, count):
    spread = jnp.broadcast_to(array[None], (count,) + array.shape)
    return lax.all_to_all(spread, axes, 0, 0, tiled=True)


def shifted(array, axis, by):
    length = lax.axis_size(axis)
    return lax.ppermute(array, axis, [(i, (i + by) % length) for i in range(length)])


def on_device(features, scaling, signal):
    yh, z, x, co, yl = (lax.axis_index(a) for a in AXES)
    lower = yl == 0
    offsets = (0, 4, -2, 2, -1, 3, 1, 5)
    place = [(yh * 4 + x) * 256 + yl * 128, co] + [(z + o) % 8 for o in offsets]
    place = jnp.stack(place).astype(jnp.int32)

    def ordered(a, b, axis):
        return jnp.concatenate([jnp.where(lower, a, b), jnp.where(lower, b, a)], axis=axis)

    give, kept = share(features, signal)
    spread = pack(features, scaling.reshape(2, 128), give)
    rows_raw = lax.all_to_all(spread, PLANE, 0, 0, tiled=True)

    got = swapped(give, "yl")
    own_scaling = jnp.where(lower, scaling[:128], scaling[128:])
    both = ordered(kept, got, 1)
    filler = jnp.zeros((EXTRA - 32, 256), F32).at[0, :128].set(own_scaling)
    own = jnp.concatenate([both[:32], filler, both[32:]], axis=0)[None]

    opposite = shifted(own, "z", 4)
    ahead, behind = shifted(own, "z", 2), shifted(own, "z", -2)
    pair = jnp.concatenate([own, opposite], axis=0)
    up, down = shifted(pair, "z", 1), shifted(pair, "z", -1)
    cols_near = jnp.concatenate([pair, ahead, behind, up, down], axis=0)
    cols_far = swapped(cols_near, "co")

    rows, scale = prepare_rows(rows_raw)
    unit0, near = tile(place, rows, cols_near, scale)
    unit1, parts = tile(place, rows, cols_far, scale, near)

    parts = lax.all_to_all(parts, LINE, 0, 0, tiled=True)
    terms, own_balanced = diffuse(place, parts, cols_near, cols_far, rows, unit0, unit1)
    other_balanced = swapped(own_balanced, "yl")
    arrived = lax.all_to_all(terms, PLANE, 0, 0, tiled=True)
    return arrived.sum(0) * ordered(own_balanced, other_balanced, 1)


def solution(mesh):
    fine = Mesh(mesh.devices.reshape(2, 8, 4, 2, 2), AXES)
    blk = ("yh", "z", "x", "co")
    return jax.shard_map(
        on_device,
        mesh=fine,
        in_specs=(P(blk, "yl"), P(blk), P("yl", blk)),
        out_specs=P("yl", blk),
        check_vma=False,
    )
```

```python
import functools
import math

import jax
import jax.numpy as jnp
from jax import lax
from jax.experimental import pallas as pl
from jax.experimental.pallas import tpu as pltpu
from jax.sharding import Mesh
from jax.sharding import PartitionSpec as P

F32, BF16 = jnp.float32, jnp.bfloat16
LOG2E = 1.4426950408889634
SHARPNESS = 48.0
NT = (((1,), (1,)), ((), ()))
NN = (((1,), (0,)), ((), ()))
SM = pl.BlockSpec(memory_space=pltpu.SMEM)
AXES = ("yh", "z", "x", "co", "yl")
PLANE = ("yh", "x", "yl")
LINE = ("z", "co")
EXTRA = 40


def params(mib):
    return pltpu.CompilerParams(vmem_limit_bytes=mib * 2**20)


def split(value):
    high = value.astype(BF16)
    return high, (value - high.astype(F32)).astype(BF16)


def unit(full):
    mean_square = jnp.mean(full * full, axis=1, keepdims=True)
    return full * (lax.rsqrt(mean_square + 1e-06) * math.sqrt(SHARPNESS / full.shape[1]))


def whole(*shape):
    return pl.BlockSpec(shape, lambda i: (0,) * len(shape))


def share_kernel(features_ref, signal_ref, give_ref, kept_ref):
    place = lax.axis_index("yl")
    for own in range(2):

        @pl.when(place == own)
        def _():
            for half, out in ((own, kept_ref), (1 - own, give_ref)):
                out[0:32, :] = signal_ref[:, half * 128 : (half + 1) * 128]
                out[32:160, :] = features_ref[half * 128 : (half + 1) * 128, :]


def share(features, signal):
    return pl.pallas_call(
        share_kernel,
        grid=(1,),
        in_specs=[whole(256, 128), whole(32, 256)],
        out_specs=[whole(160, 128)] * 2,
        out_shape=[jax.ShapeDtypeStruct((160, 128), F32)] * 2,
        compiler_params=params(62),
        cost_estimate=pl.CostEstimate(flops=100_000, bytes_accessed=300_000, transcendentals=0),
        name="share",
    )(features, signal)


def pack_kernel(features_ref, scaling_ref, after_ref, spread_ref, message_ref, sems):
    message_ref[0:256, :] = features_ref[...]
    message_ref[256:258, :] = scaling_ref[...]
    message_ref[258:264, :] = jnp.zeros((6, 128), F32)
    copies = [pltpu.make_async_copy(message_ref, spread_ref.at[n], sems.at[n]) for n in range(16)]
    for copy in copies:
        copy.start()
    for copy in copies:
        copy.wait()


def pack(features, scaling, after):
    return pl.pallas_call(
        pack_kernel,
        grid=(1,),
        in_specs=[whole(256, 128), whole(2, 128), pl.BlockSpec(memory_space=pl.ANY)],
        out_specs=pl.BlockSpec(memory_space=pltpu.HBM),
        out_shape=pltpu.HBM((16, 264, 128), F32),
        scratch_shapes=[pltpu.VMEM((264, 128), F32), pltpu.SemaphoreType.DMA((16,))],
        compiler_params=params(62),
        cost_estimate=pl.CostEstimate(flops=100_000, bytes_accessed=2_500_000, transcendentals=0),
        name="pack",
    )(features, scaling, after)


def block_rows(first, second):
    high, low = split(unit(jnp.concatenate([first[0:256, :], second[0:256, :]], axis=1)))
    return jnp.concatenate([high, low, high], axis=1)


def kernel_of(units, rows, own=None):
    kern = jnp.exp2(lax.dot_general(units, rows, NT, preferred_element_type=F32))
    if own is None:
        return kern
    col = lax.broadcasted_iota(jnp.int32, (128, 256), 0)
    row = lax.broadcasted_iota(jnp.int32, (128, 256), 1) - own
    return jnp.concatenate([jnp.where(row == col, 0.0, kern[:128]), kern[128:]], axis=0)


def tile_columns(place_ref, rows_ref, cols_ref, scale_ref, unit_ref, acc_ref, got_ref=None):
    has_self = got_ref is not None
    for b in range(8):
        high, low = split(unit(cols_ref[b, EXTRA:, :]) * LOG2E)
        at = slice(b * 128, (b + 1) * 128)
        unit_ref[at, 0:256] = high
        unit_ref[at, 256:512] = high
        unit_ref[at, 512:768] = low
    for c in range(8):
        at = slice(c * 256, (c + 1) * 256)
        if has_self:
            rows_ref[at, :] = block_rows(got_ref[2 * c], got_ref[2 * c + 1])
            scale_ref[2 * c : 2 * c + 2, :] = got_ref[2 * c, 256:258, :]
        kern = kernel_of(unit_ref[...], rows_ref[at, :], place_ref[0] - c * 256 if has_self else None)
        part = kern[:, :128] * scale_ref[2 * c : 2 * c + 1, :]
        part += kern[:, 128:] * scale_ref[2 * c + 1 : 2 * c + 2, :]
        acc_ref[...] = part if c == 0 else acc_ref[...] + part
    total = lax.dot_general(
        jnp.ones((8, 128), F32), acc_ref[...], NT, precision=lax.Precision.HIGHEST, preferred_element_type=F32
    )
    return [total[0:1, b * 128 : (b + 1) * 128] for b in range(8)]


def near_kernel(place_ref, got_ref, cols_ref, unit_ref, extra_ref, sum_ref, rows_ref, scale_ref, acc_ref):
    extra_ref[...] = cols_ref[:, 0:EXTRA, :]
    sums = tile_columns(place_ref, rows_ref, cols_ref, scale_ref, unit_ref, acc_ref, got_ref)
    for b in range(8):
        sum_ref[b : b + 1, :] = sums[b]


def far_kernel(place_ref, rows_ref, cols_ref, scale_ref, near_ref, unit_ref, extra_ref, spread_ref, acc_ref):
    extra_ref[...] = cols_ref[:, 0:EXTRA, :]
    sums = tile_columns(place_ref, rows_ref, cols_ref, scale_ref, unit_ref, acc_ref)
    first = place_ref[1] * 8
    for b in range(8):
        spread_ref[0, pl.ds(first + place_ref[2 + b], 1), :] = near_ref[b : b + 1, :]
        spread_ref[0, pl.ds(8 - first + place_ref[2 + b], 1), :] = sums[b]
    for n in range(1, 16):
        spread_ref[n] = spread_ref[0]


def tile(kernel, place, *arrays):
    vm = pl.BlockSpec(memory_space=pltpu.VMEM)
    shapes = [((1024, 768), BF16), ((8, EXTRA, 256), F32)]
    if kernel is near_kernel:
        shapes += [((8, 128), F32), ((2048, 768), BF16), ((16, 128), F32)]
    else:
        shapes += [((16, 16, 128), F32)]
    return pl.pallas_call(
        kernel,
        in_specs=[SM] + [vm] * len(arrays),
        out_specs=[vm] * len(shapes),
        out_shape=[jax.ShapeDtypeStruct(*shape) for shape in shapes],
        scratch_shapes=[pltpu.VMEM((1024, 128), F32)],
        compiler_params=params(16),
        cost_estimate=pl.CostEstimate(flops=3_200_000_000, bytes_accessed=14_000_000, transcendentals=2_000_000),
        name="tile_near" if kernel is near_kernel else "tile_far",
    )(place, *arrays)


def diffuse_kernel(
    place_ref, parts_ref, extra0, extra1, rows_ref, unit0, unit1, out_ref, balanced_ref, weight_ref, sums_ref, held
):
    for c in range(9):
        if c < 8:
            rows = rows_ref[c * 256 : (c + 1) * 256, :]
            for core, units in enumerate((unit0, unit1)):
                at = slice(core * 1024, (core + 1) * 1024)
                kern = kernel_of(units[...], rows, None if core else place_ref[0] - c * 256)
                held[c % 2, 0, at, :], held[c % 2, 1, at, :] = split(kern)
        if c == 0:
            sums_ref[...] = parts_ref[...].sum(0)
            first = place_ref[1] * 8
            for core, extra in enumerate((extra0, extra1)):
                base = first if core == 0 else 8 - first
                for b in range(8):
                    balanced = jnp.sqrt(extra[b, 32:33, 0:128] / sums_ref[pl.ds(base + place_ref[2 + b], 1), :])
                    if core == 0 and b == 0:
                        balanced_ref[...] = balanced
                    signal = jnp.concatenate([extra[b, 0:32, 0:128], extra[b, 0:32, 128:256]], axis=0)
                    start = core * 1024 + b * 128
                    for n, part in enumerate(split(signal * balanced)):
                        weight_ref[n * 64 : (n + 1) * 64, start : start + 128] = part
        if c > 0:
            slot = (c - 1) % 2
            lead = lax.dot_general(weight_ref[...], held[slot, 0], NN, preferred_element_type=F32)
            rest = lax.dot_general(weight_ref[0:64, :], held[slot, 1], NN, preferred_element_type=F32)
            total = lead[:64] + lead[64:] + rest
            out_ref[2 * c - 2] = total[:32]
            out_ref[2 * c - 1] = total[32:]


def diffuse(place, parts, extra0, extra1, rows, unit0, unit1):
    vm = pl.BlockSpec(memory_space=pltpu.VMEM)
    return pl.pallas_call(
        diffuse_kernel,
        in_specs=[SM] + [vm] * 6,
        out_specs=[vm, vm],
        out_shape=[jax.ShapeDtypeStruct((16, 32, 256), F32), jax.ShapeDtypeStruct((1, 128), F32)],
        scratch_shapes=[
            pltpu.VMEM((128, 2048), BF16),
            pltpu.VMEM((16, 128), F32),
            pltpu.VMEM((2, 2, 2048, 256), BF16),
        ],
        compiler_params=params(28),
        cost_estimate=pl.CostEstimate(flops=3_200_000_000, bytes_accessed=18_000_000, transcendentals=0),
        name="diffuse",
    )(place, parts, extra0, extra1, rows, unit0, unit1)


def swapped(array, axis):
    return lax.ppermute(array, axis, [(0, 1), (1, 0)])


def to_all(array, axes, count):
    spread = jnp.broadcast_to(array[None], (count,) + array.shape)
    return lax.all_to_all(spread, axes, 0, 0, tiled=True)


def shifted(array, axis, by):
    length = lax.axis_size(axis)
    return lax.ppermute(array, axis, [(i, (i + by) % length) for i in range(length)])


def on_device(features, scaling, signal):
    yh, z, x, co, yl = (lax.axis_index(a) for a in AXES)
    lower = yl == 0
    offsets = (0, 4, -2, 2, -1, 3, 1, 5)
    place = [(yh * 4 + x) * 256 + yl * 128, co] + [(z + o) % 8 for o in offsets]
    place = jnp.stack(place).astype(jnp.int32)

    def ordered(a, b, axis):
        return jnp.concatenate([jnp.where(lower, a, b), jnp.where(lower, b, a)], axis=axis)

    give, kept = share(features, signal)
    spread = pack(features, scaling.reshape(2, 128), give)
    rows_raw = lax.all_to_all(spread, PLANE, 0, 0, tiled=True)

    got = swapped(give, "yl")
    own_scaling = jnp.where(lower, scaling[:128], scaling[128:])
    both = ordered(kept, got, 1)
    filler = jnp.zeros((EXTRA - 32, 256), F32).at[0, :128].set(own_scaling)
    own = jnp.concatenate([both[:32], filler, both[32:]], axis=0)[None]

    opposite = shifted(own, "z", 4)
    ahead, behind = shifted(own, "z", 2), shifted(own, "z", -2)
    pair = jnp.concatenate([own, opposite], axis=0)
    up, down = shifted(pair, "z", 1), shifted(pair, "z", -1)
    cols_near = jnp.concatenate([pair, ahead, behind, up, down], axis=0)
    cols_far = swapped(cols_near, "co")

    unit0, extra0, near, rows, scale = tile(near_kernel, place, rows_raw, cols_near)
    unit1, extra1, parts = tile(far_kernel, place, rows, cols_far, scale, near)

    parts = lax.all_to_all(parts, LINE, 0, 0, tiled=True)
    terms, own_balanced = diffuse(place, parts, extra0, extra1, rows, unit0, unit1)
    other_balanced = swapped(own_balanced, "yl")
    arrived = lax.all_to_all(terms, PLANE, 0, 0, tiled=True)
    return arrived.sum(0) * ordered(own_balanced, other_balanced, 1)


def solution(mesh):
    fine = Mesh(mesh.devices.reshape(2, 8, 4, 2, 2), AXES)
    blk = ("yh", "z", "x", "co")
    return jax.shard_map(
        on_device,
        mesh=fine,
        in_specs=(P(blk, "yl"), P(blk), P("yl", blk)),
        out_specs=P("yl", blk),
        check_vma=False,
    )
```

```python
import functools
import math

import jax
import jax.numpy as jnp
from jax import lax
from jax.experimental import pallas as pl
from jax.experimental.pallas import tpu as pltpu
from jax.sharding import Mesh
from jax.sharding import PartitionSpec as P

F32, BF16 = jnp.float32, jnp.bfloat16
LOG2E = 1.4426950408889634
SHARPNESS = 48.0
NT = (((1,), (1,)), ((), ()))
NN = (((1,), (0,)), ((), ()))
SM = pl.BlockSpec(memory_space=pltpu.SMEM)
AXES = ("yh", "z", "x", "co", "yl")
PLANE = ("yh", "x", "yl")
LINE = ("z", "co")
EXTRA = 40


def params(mib):
    return pltpu.CompilerParams(vmem_limit_bytes=mib * 2**20)


def split(value):
    high = value.astype(BF16)
    return high, (value - high.astype(F32)).astype(BF16)


def unit(full):
    mean_square = jnp.mean(full * full, axis=1, keepdims=True)
    return full * (lax.rsqrt(mean_square + 1e-06) * math.sqrt(SHARPNESS / full.shape[1]))


def whole(*shape):
    return pl.BlockSpec(shape, lambda i: (0,) * len(shape))


def pack_kernel(features_ref, scaling_ref, signal_ref, spread_ref, give_ref, kept_ref, message_ref, sems):
    message_ref[0:256, :] = features_ref[...]
    message_ref[256:258, :] = scaling_ref[...]
    message_ref[258:264, :] = jnp.zeros((6, 128), F32)
    copies = [pltpu.make_async_copy(message_ref, spread_ref.at[n], sems.at[n]) for n in range(16)]
    for copy in copies:
        copy.start()
    place = lax.axis_index("yl")
    for own in range(2):

        @pl.when(place == own)
        def _():
            for half, out in ((own, kept_ref), (1 - own, give_ref)):
                out[0:32, :] = signal_ref[:, half * 128 : (half + 1) * 128]
                out[32:160, :] = features_ref[half * 128 : (half + 1) * 128, :]

    for copy in copies:
        copy.wait()


def pack(features, scaling, signal):
    return pl.pallas_call(
        pack_kernel,
        grid=(1,),
        in_specs=[whole(256, 128), whole(2, 128), whole(32, 256)],
        out_specs=[pl.BlockSpec(memory_space=pltpu.HBM), whole(160, 128), whole(160, 128)],
        out_shape=[pltpu.HBM((16, 264, 128), F32)] + [jax.ShapeDtypeStruct((160, 128), F32)] * 2,
        scratch_shapes=[pltpu.VMEM((264, 128), F32), pltpu.SemaphoreType.DMA((16,))],
        compiler_params=params(62),
        cost_estimate=pl.CostEstimate(flops=100_000, bytes_accessed=2_500_000, transcendentals=0),
        name="pack",
    )(features, scaling, signal)


def gate_kernel(spread_ref, after_ref, out_ref):
    pass


def gate(spread, after):
    hbm = pl.BlockSpec(memory_space=pltpu.HBM)
    return pl.pallas_call(
        gate_kernel,
        in_specs=[hbm, pl.BlockSpec(memory_space=pl.ANY)],
        out_specs=hbm,
        out_shape=pltpu.HBM(spread.shape, F32),
        input_output_aliases={0: 0},
        compiler_params=params(62),
        cost_estimate=pl.CostEstimate(flops=100_000, bytes_accessed=2_500_000, transcendentals=0),
        name="gate",
    )(spread, after)


def block_rows(first, second):
    high, low = split(unit(jnp.concatenate([first[0:256, :], second[0:256, :]], axis=1)))
    return jnp.concatenate([high, low, high], axis=1)


def kernel_of(units, rows, own=None):
    kern = jnp.exp2(lax.dot_general(units, rows, NT, preferred_element_type=F32))
    if own is None:
        return kern
    col = lax.broadcasted_iota(jnp.int32, (128, 256), 0)
    row = lax.broadcasted_iota(jnp.int32, (128, 256), 1) - own
    return jnp.concatenate([jnp.where(row == col, 0.0, kern[:128]), kern[128:]], axis=0)


def tile_columns(place_ref, rows_ref, cols_ref, scale_ref, unit_ref, acc_ref, got_ref=None):
    has_self = got_ref is not None
    for b in range(8):
        high, low = split(unit(cols_ref[b, EXTRA:, :]) * LOG2E)
        at = slice(b * 128, (b + 1) * 128)
        unit_ref[at, 0:256] = high
        unit_ref[at, 256:512] = high
        unit_ref[at, 512:768] = low
    for c in range(8):
        at = slice(c * 256, (c + 1) * 256)
        if has_self:
            rows_ref[at, :] = block_rows(got_ref[2 * c], got_ref[2 * c + 1])
            scale_ref[2 * c : 2 * c + 2, :] = got_ref[2 * c, 256:258, :]
        kern = kernel_of(unit_ref[...], rows_ref[at, :], place_ref[0] - c * 256 if has_self else None)
        part = kern[:, :128] * scale_ref[2 * c : 2 * c + 1, :]
        part += kern[:, 128:] * scale_ref[2 * c + 1 : 2 * c + 2, :]
        acc_ref[...] = part if c == 0 else acc_ref[...] + part
    total = lax.dot_general(
        jnp.ones((8, 128), F32), acc_ref[...], NT, precision=lax.Precision.HIGHEST, preferred_element_type=F32
    )
    return [total[0:1, b * 128 : (b + 1) * 128] for b in range(8)]


def near_kernel(place_ref, got_ref, cols_ref, unit_ref, extra_ref, sum_ref, rows_ref, scale_ref, acc_ref):
    extra_ref[...] = cols_ref[:, 0:EXTRA, :]
    sums = tile_columns(place_ref, rows_ref, cols_ref, scale_ref, unit_ref, acc_ref, got_ref)
    for b in range(8):
        sum_ref[b : b + 1, :] = sums[b]


def far_kernel(place_ref, rows_ref, cols_ref, scale_ref, near_ref, unit_ref, extra_ref, spread_ref, acc_ref):
    extra_ref[...] = cols_ref[:, 0:EXTRA, :]
    sums = tile_columns(place_ref, rows_ref, cols_ref, scale_ref, unit_ref, acc_ref)
    first = place_ref[1] * 8
    for b in range(8):
        spread_ref[0, pl.ds(first + place_ref[2 + b], 1), :] = near_ref[b : b + 1, :]
        spread_ref[0, pl.ds(8 - first + place_ref[2 + b], 1), :] = sums[b]
    for n in range(1, 16):
        spread_ref[n] = spread_ref[0]


def tile(kernel, place, *arrays):
    vm = pl.BlockSpec(memory_space=pltpu.VMEM)
    shapes = [((1024, 768), BF16), ((8, EXTRA, 256), F32)]
    if kernel is near_kernel:
        shapes += [((8, 128), F32), ((2048, 768), BF16), ((16, 128), F32)]
    else:
        shapes += [((16, 16, 128), F32)]
    return pl.pallas_call(
        kernel,
        in_specs=[SM] + [vm] * len(arrays),
        out_specs=[vm] * len(shapes),
        out_shape=[jax.ShapeDtypeStruct(*shape) for shape in shapes],
        scratch_shapes=[pltpu.VMEM((1024, 128), F32)],
        compiler_params=params(16),
        cost_estimate=pl.CostEstimate(flops=3_200_000_000, bytes_accessed=14_000_000, transcendentals=2_000_000),
        name="tile_near" if kernel is near_kernel else "tile_far",
    )(place, *arrays)


def diffuse_kernel(
    place_ref, parts_ref, extra0, extra1, rows_ref, unit0, unit1,
    terms_ref, balanced_ref, weight_ref, sums_ref, held, out_ref, sems,
):
    copies = []
    for c in range(9):
        if c < 8:
            rows = rows_ref[c * 256 : (c + 1) * 256, :]
            for core, units in enumerate((unit0, unit1)):
                at = slice(core * 1024, (core + 1) * 1024)
                kern = kernel_of(units[...], rows, None if core else place_ref[0] - c * 256)
                held[c % 2, 0, at, :], held[c % 2, 1, at, :] = split(kern)
        if c == 0:
            sums_ref[...] = parts_ref[...].sum(0)
            first = place_ref[1] * 8
            for core, extra in enumerate((extra0, extra1)):
                base = first if core == 0 else 8 - first
                for b in range(8):
                    balanced = jnp.sqrt(extra[b, 32:33, 0:128] / sums_ref[pl.ds(base + place_ref[2 + b], 1), :])
                    if core == 0 and b == 0:
                        balanced_ref[...] = balanced
                    signal = jnp.concatenate([extra[b, 0:32, 0:128], extra[b, 0:32, 128:256]], axis=0)
                    start = core * 1024 + b * 128
                    for n, part in enumerate(split(signal * balanced)):
                        weight_ref[n * 64 : (n + 1) * 64, start : start + 128] = part
        if c > 0:
            slot = (c - 1) % 2
            lead = lax.dot_general(weight_ref[...], held[slot, 0], NN, preferred_element_type=F32)
            rest = lax.dot_general(weight_ref[0:64, :], held[slot, 1], NN, preferred_element_type=F32)
            total = lead[:64] + lead[64:] + rest
            out_ref[2 * c - 2] = total[:32]
            out_ref[2 * c - 1] = total[32:]
            pair = pl.ds(2 * c - 2, 2)
            copies.append(pltpu.make_async_copy(out_ref.at[pair], terms_ref.at[pair], sems.at[c - 1]))
            copies[-1].start()
    for copy in copies:
        copy.wait()


def diffuse(place, parts, extra0, extra1, rows, unit0, unit1):
    vm = pl.BlockSpec(memory_space=pltpu.VMEM)
    return pl.pallas_call(
        diffuse_kernel,
        in_specs=[SM] + [vm] * 6,
        out_specs=[pl.BlockSpec(memory_space=pltpu.HBM), vm],
        out_shape=[pltpu.HBM((16, 32, 256), F32), jax.ShapeDtypeStruct((1, 128), F32)],
        scratch_shapes=[
            pltpu.VMEM((128, 2048), BF16),
            pltpu.VMEM((16, 128), F32),
            pltpu.VMEM((2, 2, 2048, 256), BF16),
            pltpu.VMEM((16, 32, 256), F32),
            pltpu.SemaphoreType.DMA((8,)),
        ],
        compiler_params=params(28),
        cost_estimate=pl.CostEstimate(flops=3_200_000_000, bytes_accessed=18_000_000, transcendentals=0),
        name="diffuse",
    )(place, parts, extra0, extra1, rows, unit0, unit1)


def swapped(array, axis):
    return lax.ppermute(array, axis, [(0, 1), (1, 0)])


def to_all(array, axes, count):
    spread = jnp.broadcast_to(array[None], (count,) + array.shape)
    return lax.all_to_all(spread, axes, 0, 0, tiled=True)


def shifted(array, axis, by):
    length = lax.axis_size(axis)
    return lax.ppermute(array, axis, [(i, (i + by) % length) for i in range(length)])


def on_device(features, scaling, signal):
    yh, z, x, co, yl = (lax.axis_index(a) for a in AXES)
    lower = yl == 0
    offsets = (0, 4, -2, 2, -1, 3, 1, 5)
    place = [(yh * 4 + x) * 256 + yl * 128, co] + [(z + o) % 8 for o in offsets]
    place = jnp.stack(place).astype(jnp.int32)

    def ordered(a, b, axis):
        return jnp.concatenate([jnp.where(lower, a, b), jnp.where(lower, b, a)], axis=axis)

    spread, give, kept = pack(features, scaling.reshape(2, 128), signal)
    spread = gate(spread, give)
    rows_raw = lax.all_to_all(spread, PLANE, 0, 0, tiled=True)

    got = swapped(give, "yl")
    own_scaling = jnp.where(lower, scaling[:128], scaling[128:])
    both = ordered(kept, got, 1)
    filler = jnp.zeros((EXTRA - 32, 256), F32).at[0, :128].set(own_scaling)
    own = jnp.concatenate([both[:32], filler, both[32:]], axis=0)[None]

    opposite = shifted(own, "z", 4)
    ahead, behind = shifted(own, "z", 2), shifted(own, "z", -2)
    pair = jnp.concatenate([own, opposite], axis=0)
    up, down = shifted(pair, "z", 1), shifted(pair, "z", -1)
    cols_near = jnp.concatenate([pair, ahead, behind, up, down], axis=0)
    cols_far = swapped(cols_near, "co")

    unit0, extra0, near, rows, scale = tile(near_kernel, place, rows_raw, cols_near)
    unit1, extra1, parts = tile(far_kernel, place, rows, cols_far, scale, near)

    parts = lax.all_to_all(parts, LINE, 0, 0, tiled=True)
    terms, own_balanced = diffuse(place, parts, extra0, extra1, rows, unit0, unit1)
    other_balanced = swapped(own_balanced, "yl")
    arrived = lax.all_to_all(terms, PLANE, 0, 0, tiled=True)
    return arrived.sum(0) * ordered(own_balanced, other_balanced, 1)


def solution(mesh):
    fine = Mesh(mesh.devices.reshape(2, 8, 4, 2, 2), AXES)
    blk = ("yh", "z", "x", "co")
    return jax.shard_map(
        on_device,
        mesh=fine,
        in_specs=(P(blk, "yl"), P(blk), P("yl", blk)),
        out_specs=P("yl", blk),
        check_vma=False,
    )
```

```python
import functools
import math

import jax
import jax.numpy as jnp
from jax import lax
from jax.experimental import pallas as pl
from jax.experimental.pallas import tpu as pltpu
from jax.sharding import Mesh
from jax.sharding import PartitionSpec as P

F32, BF16 = jnp.float32, jnp.bfloat16
LOG2E = 1.4426950408889634
SHARPNESS = 48.0
NT = (((1,), (1,)), ((), ()))
NN = (((1,), (0,)), ((), ()))
SM = pl.BlockSpec(memory_space=pltpu.SMEM)
AXES = ("yh", "z", "x", "co", "yl")
PLANE = ("yh", "x", "yl")
LINE = ("z", "co")
EXTRA = 40


def params(mib):
    return pltpu.CompilerParams(vmem_limit_bytes=mib * 2**20)


def split(value):
    high = value.astype(BF16)
    return high, (value - high.astype(F32)).astype(BF16)


def unit(full):
    mean_square = jnp.mean(full * full, axis=1, keepdims=True)
    return full * (lax.rsqrt(mean_square + 1e-06) * math.sqrt(SHARPNESS / full.shape[1]))


def whole(*shape):
    return pl.BlockSpec(shape, lambda i: (0,) * len(shape))


def pack_kernel(features_ref, scaling_ref, signal_ref, spread_ref, give_ref, kept_ref, message_ref, sems):
    message_ref[0:256, :] = features_ref[...]
    message_ref[256:258, :] = scaling_ref[...]
    message_ref[258:264, :] = jnp.zeros((6, 128), F32)
    copies = [pltpu.make_async_copy(message_ref, spread_ref.at[n], sems.at[n]) for n in range(16)]
    for copy in copies:
        copy.start()
    place = lax.axis_index("yl")
    for own in range(2):

        @pl.when(place == own)
        def _():
            for half, out in ((own, kept_ref), (1 - own, give_ref)):
                out[0:32, :] = signal_ref[:, half * 128 : (half + 1) * 128]
                out[32:160, :] = features_ref[half * 128 : (half + 1) * 128, :]

    for copy in copies:
        copy.wait()


def pack(features, scaling, signal):
    return pl.pallas_call(
        pack_kernel,
        grid=(1,),
        in_specs=[whole(256, 128), whole(2, 128), whole(32, 256)],
        out_specs=[pl.BlockSpec(memory_space=pltpu.HBM), whole(160, 128), whole(160, 128)],
        out_shape=[pltpu.HBM((16, 264, 128), F32)] + [jax.ShapeDtypeStruct((160, 128), F32)] * 2,
        scratch_shapes=[pltpu.VMEM((264, 128), F32), pltpu.SemaphoreType.DMA((16,))],
        compiler_params=params(62),
        cost_estimate=pl.CostEstimate(flops=100_000, bytes_accessed=2_500_000, transcendentals=0),
        name="pack",
    )(features, scaling, signal)


def gate_kernel(spread_ref, after_ref, out_ref):
    pass


def gate(spread, after):
    hbm = pl.BlockSpec(memory_space=pltpu.HBM)
    return pl.pallas_call(
        gate_kernel,
        in_specs=[hbm, pl.BlockSpec(memory_space=pl.ANY)],
        out_specs=hbm,
        out_shape=pltpu.HBM(spread.shape, F32),
        input_output_aliases={0: 0},
        compiler_params=params(62),
        cost_estimate=pl.CostEstimate(flops=100_000, bytes_accessed=2_500_000, transcendentals=0),
        name="gate",
    )(spread, after)


def block_rows(first, second):
    high, low = split(unit(jnp.concatenate([first[0:256, :], second[0:256, :]], axis=1)))
    return jnp.concatenate([high, low, high], axis=1)


def kernel_of(units, rows, own=None):
    kern = jnp.exp2(lax.dot_general(units, rows, NT, preferred_element_type=F32))
    if own is None:
        return kern
    col = lax.broadcasted_iota(jnp.int32, (128, 256), 0)
    row = lax.broadcasted_iota(jnp.int32, (128, 256), 1) - own
    return jnp.concatenate([jnp.where(row == col, 0.0, kern[:128]), kern[128:]], axis=0)


def tile_columns(place_ref, rows_ref, cols_ref, scale_ref, unit_ref, acc_ref, got_ref=None):
    has_self = got_ref is not None
    for b in range(8):
        high, low = split(unit(cols_ref[b, EXTRA:, :]) * LOG2E)
        at = slice(b * 128, (b + 1) * 128)
        unit_ref[at, 0:256] = high
        unit_ref[at, 256:512] = high
        unit_ref[at, 512:768] = low
    for c in range(8):
        at = slice(c * 256, (c + 1) * 256)
        if has_self:
            rows_ref[at, :] = block_rows(got_ref[2 * c], got_ref[2 * c + 1])
            scale_ref[2 * c : 2 * c + 2, :] = got_ref[2 * c, 256:258, :]
        kern = kernel_of(unit_ref[...], rows_ref[at, :], place_ref[0] - c * 256 if has_self else None)
        part = kern[:, :128] * scale_ref[2 * c : 2 * c + 1, :]
        part += kern[:, 128:] * scale_ref[2 * c + 1 : 2 * c + 2, :]
        acc_ref[...] = part if c == 0 else acc_ref[...] + part
    total = lax.dot_general(
        jnp.ones((8, 128), F32), acc_ref[...], NT, precision=lax.Precision.HIGHEST, preferred_element_type=F32
    )
    return [total[0:1, b * 128 : (b + 1) * 128] for b in range(8)]


def near_kernel(place_ref, got_ref, cols_ref, unit_ref, extra_ref, sum_ref, rows_ref, scale_ref, acc_ref):
    extra_ref[...] = cols_ref[:, 0:EXTRA, :]
    sums = tile_columns(place_ref, rows_ref, cols_ref, scale_ref, unit_ref, acc_ref, got_ref)
    for b in range(8):
        sum_ref[b : b + 1, :] = sums[b]


def far_kernel(place_ref, rows_ref, cols_ref, scale_ref, near_ref, unit_ref, extra_ref, spread_ref, acc_ref):
    extra_ref[...] = cols_ref[:, 0:EXTRA, :]
    sums = tile_columns(place_ref, rows_ref, cols_ref, scale_ref, unit_ref, acc_ref)
    first = place_ref[1] * 8
    for b in range(8):
        spread_ref[0, pl.ds(first + place_ref[2 + b], 1), :] = near_ref[b : b + 1, :]
        spread_ref[0, pl.ds(8 - first + place_ref[2 + b], 1), :] = sums[b]
    for n in range(1, 16):
        spread_ref[n] = spread_ref[0]


def tile(kernel, place, *arrays):
    vm = pl.BlockSpec(memory_space=pltpu.VMEM)
    shapes = [((1024, 768), BF16), ((8, EXTRA, 256), F32)]
    if kernel is near_kernel:
        shapes += [((8, 128), F32), ((2048, 768), BF16), ((16, 128), F32)]
    else:
        shapes += [((16, 16, 128), F32)]
    return pl.pallas_call(
        kernel,
        in_specs=[SM] + [vm] * len(arrays),
        out_specs=[vm] * len(shapes),
        out_shape=[jax.ShapeDtypeStruct(*shape) for shape in shapes],
        scratch_shapes=[pltpu.VMEM((1024, 128), F32)],
        compiler_params=params(16),
        cost_estimate=pl.CostEstimate(flops=3_200_000_000, bytes_accessed=14_000_000, transcendentals=2_000_000),
        name="tile_near" if kernel is near_kernel else "tile_far",
    )(place, *arrays)


def diffuse_kernel(
    place_ref, parts_ref, extra0, extra1, rows_ref, unit0, unit1,
    terms_ref, balanced_ref, weight_ref, sums_ref, held, out_ref, sems,
):
    copies = []
    for c in range(9):
        if c < 8:
            rows = rows_ref[c * 256 : (c + 1) * 256, :]
            for core, units in enumerate((unit0, unit1)):
                at = slice(core * 1024, (core + 1) * 1024)
                kern = kernel_of(units[...], rows, None if core else place_ref[0] - c * 256)
                held[c % 2, 0, at, :], held[c % 2, 1, at, :] = split(kern)
        if c == 0:
            sums_ref[...] = parts_ref[...].sum(0)
            first = place_ref[1] * 8
            for core, extra in enumerate((extra0, extra1)):
                base = first if core == 0 else 8 - first
                for b in range(8):
                    balanced = jnp.sqrt(extra[b, 32:33, 0:128] / sums_ref[pl.ds(base + place_ref[2 + b], 1), :])
                    if core == 0 and b == 0:
                        balanced_ref[...] = balanced
                    signal = jnp.concatenate([extra[b, 0:32, 0:128], extra[b, 0:32, 128:256]], axis=0)
                    start = core * 1024 + b * 128
                    for n, part in enumerate(split(signal * balanced)):
                        weight_ref[n * 64 : (n + 1) * 64, start : start + 128] = part
        if c > 0:
            slot = (c - 1) % 2
            lead = lax.dot_general(weight_ref[...], held[slot, 0], NN, preferred_element_type=F32)
            rest = lax.dot_general(weight_ref[0:64, :], held[slot, 1], NN, preferred_element_type=F32)
            total = lead[:64] + lead[64:] + rest
            out_ref[2 * c - 2] = total[:32]
            out_ref[2 * c - 1] = total[32:]
            pair = pl.ds(2 * c - 2, 2)
            copies.append(pltpu.make_async_copy(out_ref.at[pair], terms_ref.at[pair], sems.at[c - 1]))
            copies[-1].start()
    for copy in copies:
        copy.wait()


def diffuse(place, parts, extra0, extra1, rows, unit0, unit1):
    vm = pl.BlockSpec(memory_space=pltpu.VMEM)
    return pl.pallas_call(
        diffuse_kernel,
        in_specs=[SM] + [vm] * 6,
        out_specs=[pl.BlockSpec(memory_space=pltpu.HBM), vm],
        out_shape=[pltpu.HBM((16, 32, 256), F32), jax.ShapeDtypeStruct((1, 128), F32)],
        scratch_shapes=[
            pltpu.VMEM((128, 2048), BF16),
            pltpu.VMEM((16, 128), F32),
            pltpu.VMEM((2, 2, 2048, 256), BF16),
            pltpu.VMEM((16, 32, 256), F32),
            pltpu.SemaphoreType.DMA((8,)),
        ],
        compiler_params=params(28),
        cost_estimate=pl.CostEstimate(flops=3_200_000_000, bytes_accessed=18_000_000, transcendentals=0),
        name="diffuse",
    )(place, parts, extra0, extra1, rows, unit0, unit1)


def swapped(array, axis):
    return lax.ppermute(array, axis, [(0, 1), (1, 0)])


def to_all(array, axes, count):
    spread = jnp.broadcast_to(array[None], (count,) + array.shape)
    return lax.all_to_all(spread, axes, 0, 0, tiled=True)


def shifted(array, axis, by):
    length = lax.axis_size(axis)
    return lax.ppermute(array, axis, [(i, (i + by) % length) for i in range(length)])


def on_device(features, scaling, signal):
    yh, z, x, co, yl = (lax.axis_index(a) for a in AXES)
    lower = yl == 0
    offsets = (0, 4, -1, 1, -2, -3, 2, 3)
    place = [(yh * 4 + x) * 256 + yl * 128, co] + [(z + o) % 8 for o in offsets]
    place = jnp.stack(place).astype(jnp.int32)

    def ordered(a, b, axis):
        return jnp.concatenate([jnp.where(lower, a, b), jnp.where(lower, b, a)], axis=axis)

    spread, give, kept = pack(features, scaling.reshape(2, 128), signal)
    spread = gate(spread, give)
    rows_raw = lax.all_to_all(spread, PLANE, 0, 0, tiled=True)

    got = swapped(give, "yl")
    own_scaling = jnp.where(lower, scaling[:128], scaling[128:])
    both = ordered(kept, got, 1)
    filler = jnp.zeros((EXTRA - 32, 256), F32).at[0, :128].set(own_scaling)
    own = jnp.concatenate([both[:32], filler, both[32:]], axis=0)[None]

    up, down = shifted(own, "z", 1), shifted(own, "z", -1)
    opposite = shifted(own, "z", 4)
    ahead = shifted(jnp.concatenate([own, up], axis=0), "z", 2)
    behind = shifted(jnp.concatenate([own, down], axis=0), "z", -2)
    cols_near = jnp.concatenate([own, opposite, up, down, ahead, behind], axis=0)
    cols_far = swapped(cols_near, "co")

    unit0, extra0, near, rows, scale = tile(near_kernel, place, rows_raw, cols_near)
    unit1, extra1, parts = tile(far_kernel, place, rows, cols_far, scale, near)

    parts = lax.all_to_all(parts, LINE, 0, 0, tiled=True)
    terms, own_balanced = diffuse(place, parts, extra0, extra1, rows, unit0, unit1)
    other_balanced = swapped(own_balanced, "yl")
    arrived = lax.all_to_all(terms, PLANE, 0, 0, tiled=True)
    return arrived.sum(0) * ordered(own_balanced, other_balanced, 1)


def solution(mesh):
    fine = Mesh(mesh.devices.reshape(2, 8, 4, 2, 2), AXES)
    blk = ("yh", "z", "x", "co")
    return jax.shard_map(
        on_device,
        mesh=fine,
        in_specs=(P(blk, "yl"), P(blk), P("yl", blk)),
        out_specs=P("yl", blk),
        check_vma=False,
    )
```
